256 devices in a mesh: dp: 4 (over z_hi), space: 64 (over x, z_lo, y, core).
Axes of the slice: x: 4, y: 4, z: 8 (z_hi: 4, z_lo: 2; z = z_hi * 2 + z_lo), core: 2. Of those that a mesh axis runs over, the one named last changes fastest.
Arguments:
- density_cubes: bfloat16 [4, 4, 512, 64, 128], P('dp', None, 'space'), may hold values from -6 to 6
- first_kernel: bfloat16 [16, 4, 3, 3, 3], replicated, may hold values from -0.625 to 0.625
- second_kernel: bfloat16 [32, 16, 3, 3, 3], replicated, may hold values from -0.3125 to 0.3125
- third_kernel: bfloat16 [64, 32, 3, 3, 3], replicated, may hold values from -0.21875 to 0.21875
- cotangent: bfloat16 [4, 64, 64, 8, 16], P('dp', 'space'), may hold values from -0.03125 to 0.03125
Outputs:
- features: bfloat16 [4, 64, 64, 8, 16], P('dp', 'space')
- first_grad: float32 [16, 4, 3, 3, 3], replicated
- second_grad: float32 [32, 16, 3, 3, 3], replicated
- third_grad: float32 [64, 32, 3, 3, 3], P('space')
The draws below stay inside these ranges and needn't reach their ends.
All inputs are finite; a program needn't handle non-finite values.
Results may differ from the reference program's by a relative error of at most 0.012.
Values may be sent and summed in bfloat16 or wider, within the bound.
No kernel may reach another device: no remote copies, remote signals or barrier semaphores. Data moves between devices by JAX's collectives and lax.ppermute only.
A program may use at most 320 MiB of HBM per device.

```python
import jax
import jax.numpy as jnp
from jax import lax

C0 = 4
C1 = 16
C2 = 32
C3 = 64
NY = 64
NZ = 128
SAMPLES = 4
NX = 512


def levels(own_key, shape, split, low, high):
    factor_of = 1.0
    for axis_at, blocks in split:
        heights = jax.random.uniform(jax.random.fold_in(jax.random.fold_in(own_key, 6), axis_at), (blocks,), jnp.float32, low / len(split), high / len(split))
        factor_of = factor_of * jnp.repeat(jnp.exp(heights), shape[axis_at] // blocks).reshape((-1,) + (1,) * (len(shape) - 1 - axis_at))
    return factor_of


def noise(own_key, shape, scale, most, split=(), held_as=jnp.bfloat16):
    values = scale * jax.random.normal(own_key, shape, jnp.float32)
    if split:
        values = values * levels(own_key, shape, split, -0.22, 0.18)
    return jnp.clip(values, -most, most).astype(held_as)


def setup_inputs(seed: int = 0) -> dict:
    arg_keys = jax.random.split(jax.random.key(seed), 6)
    return {
        "density_cubes": noise(arg_keys[0], (SAMPLES, C0, NX, NY, NZ), 1.0, 6.0, ((0, 4), (2, 64))),
        "first_kernel": noise(arg_keys[1], (C1, C0, 3, 3, 3), (C0 * 27) ** -0.5, 0.625),
        "second_kernel": noise(arg_keys[2], (C2, C1, 3, 3, 3), (C1 * 27) ** -0.5, 0.3125),
        "third_kernel": noise(arg_keys[3], (C3, C2, 3, 3, 3), (C2 * 27) ** -0.5, 0.21875),
        "cotangent": noise(arg_keys[4], (SAMPLES, C3, NX // 8, NY // 8, NZ // 8), (SAMPLES * NX * NY * NZ // 512) ** -0.5, 0.03125, ((0, 4), (1, 64))),
    }


def convolve(inputs, kernel, padding):
    return lax.conv_general_dilated(inputs, kernel, (2, 2, 2), padding, dimension_numbers=('NCDHW', 'OIDHW', 'NCDHW'), preferred_element_type=jnp.float32)

def input_gradient(deltas, kernel, padding):
    flipped = kernel[:, :, ::-1, ::-1, ::-1]
    return lax.conv_general_dilated(deltas, flipped, (1, 1, 1), padding, lhs_dilation=(2, 2, 2), dimension_numbers=('NCDHW', 'IODHW', 'NCDHW'), preferred_element_type=jnp.float32)

def kernel_gradient(inputs, deltas, padding):
    result = lax.conv_general_dilated(inputs, deltas, (1, 1, 1), padding, rhs_dilation=(2, 2, 2), dimension_numbers=('CNDHW', 'IODHW', 'NCDHW'), preferred_element_type=jnp.float32)
    return jnp.transpose(result, (1, 0, 2, 3, 4))

def activate(preact):
    return jax.nn.gelu(preact, approximate=True)

def gelu_backward(preact, upstream):
    unused, pullback = jax.vjp(activate, preact)
    return pullback(upstream)[0]

def reference(density_cubes, first_kernel, second_kernel, third_kernel, cotangent):
    forward_pads = ((1, 0), (1, 0), (1, 0))
    transpose_pads = ((1, 2), (1, 2), (1, 2))
    first_pre = convolve(density_cubes, first_kernel, forward_pads)
    first_act = activate(first_pre).astype(jnp.bfloat16)
    second_pre = convolve(first_act, second_kernel, forward_pads)
    second_act = activate(second_pre).astype(jnp.bfloat16)
    third_pre = convolve(second_act, third_kernel, forward_pads)
    features = activate(third_pre).astype(jnp.bfloat16)
    delta_third = gelu_backward(third_pre, cotangent.astype(jnp.float32)).astype(jnp.bfloat16)
    third_grad = kernel_gradient(second_act, delta_third, forward_pads)
    upstream_second = input_gradient(delta_third, third_kernel, transpose_pads)
    delta_second = gelu_backward(second_pre, upstream_second).astype(jnp.bfloat16)
    second_grad = kernel_gradient(first_act, delta_second, forward_pads)
    upstream_first = input_gradient(delta_second, second_kernel, transpose_pads)
    delta_first = gelu_backward(first_pre, upstream_first).astype(jnp.bfloat16)
    first_grad = kernel_gradient(density_cubes, delta_first, forward_pads)
    return (features, first_grad, second_grad, third_grad)
```

```python
import math

import jax
import jax.numpy as jnp
import numpy as np
from jax import lax
from jax.experimental import pallas as pl
from jax.experimental.pallas import tpu as pltpu
from jax.sharding import PartitionSpec as P


BF16 = jnp.bfloat16
F32 = jnp.float32
CELLS = 128
ROWS0, ROWS1, ROWS2 = 48, 80, 96
SCALE = math.sqrt(2.0 / math.pi)
SPACE = ("x", "z", "y", "core")
NEAR = ("z", "y", "core")
FAR = ("dp", "x")


def first_selection():
    chosen = np.zeros((4, 4, 32, 9, ROWS0), np.float32)
    for ry in range(4):
        for c in range(4):
            for kx in range(3):
                for ky in range(3):
                    for kz in range(3):
                        y = 2 * ry + ky - 1
                        row = 32 + c if y < 0 else 8 * c + y
                        chosen[ry, c, 9 * kx + 3 * ky + kz, 3 * kx + kz, row] = 1
    return chosen.reshape(4, 128, 9 * ROWS0)


def dot(a, b, contract, precision=None):
    return lax.dot_general(a, b, (contract, ((), ())), preferred_element_type=F32, precision=precision)


def lane_iota(rows):
    return lax.broadcasted_iota(jnp.int32, (rows, CELLS), 1)


def up_y(block):
    return jnp.where(lane_iota(block.shape[0]) >= 16, pltpu.roll(block, 16, 1), 0.0)


def up_z(block):
    return jnp.where(lane_iota(block.shape[0]) % 16 != 0, pltpu.roll(block, 1, 1), 0.0)


def down_y(block):
    return jnp.where(lane_iota(block.shape[0]) < CELLS - 16, pltpu.roll(block, CELLS - 16, 1), 0.0)


def down_z(block):
    return jnp.where(lane_iota(block.shape[0]) % 16 != 15, pltpu.roll(block, CELLS - 1, 1), 0.0)


def gelu_and_slope(x):
    square = x * x
    t = jnp.tanh(SCALE * (x + 0.044715 * (x * square)))
    half = 0.5 * (1.0 + t)
    slope = half + 0.5 * x * (1.0 - t * t) * (SCALE * (1.0 + 3 * 0.044715 * square))
    return x * half, slope


def fill_permutation(perm_ref):
    z = lax.broadcasted_iota(jnp.int32, (CELLS, CELLS), 0)
    u = lane_iota(CELLS)
    offset = z - 8 * (u % 16)
    for zi in range(9):
        hit = offset == zi - 1
        for y in range(8):
            block = jnp.where(hit & (u // 16 == y), 1.0, 0.0)
            perm_ref[128 * y : 128 * y + 128, 128 * zi : 128 * zi + 128] = block.astype(BF16)


OWN, HALO, ABOVE = 0, 256, 480


def spread_plane(plane_ref, wide_ref, base, x):
    for c in range(4):
        plane = plane_ref[c].astype(F32)
        for y in range(8):
            tile = plane[8 * y : 8 * y + 8]
            wide_ref[base + 8 * c : base + 8 * c + 8, 128 * y : 128 * y + 128] = tile
            if y < 7:
                row = ABOVE + 4 * x + c
                wide_ref[row : row + 1, 128 * y + 128 : 128 * y + 256] = tile[7:8]


def to_cells(wide_ref, perm_ref, start, stop, planes, above, out_ref):
    rows = wide_ref[start:stop, :].astype(BF16)
    upper = lax.broadcasted_iota(jnp.int32, (8, CELLS), 0) < 4
    for first in range(0, 9, 2):
        count = min(2, 9 - first)
        got = dot(rows, perm_ref[:, 128 * first : 128 * (first + count)], ((1,), (0,)))
        for j in range(count):
            lanes = slice(128 * j, 128 * j + 128)
            base = ROWS0 * (first + j)
            for at, x in enumerate(planes):
                out_ref[x, base : base + 32, :] = got[32 * at : 32 * at + 32, lanes].astype(BF16)
            if above:
                for x in range(15):
                    at = 32 * len(planes) + 8 * (x // 2)
                    tile = got[at : at + 8, lanes]
                    tile = jnp.where(upper, tile if x % 2 == 0 else pltpu.roll(tile, 4, 0), 0.0)
                    tile = jnp.concatenate([tile, jnp.zeros((8, CELLS), F32)], axis=0)
                    out_ref[x, base + 32 : base + 48, :] = tile.astype(BF16)


def arrange_kernels(k1_ref, k2_ref, k3_ref, chosen_ref, k1_scratch, w1_ref, w2_ref, w3_ref):
    k1_scratch[...] = k1_ref[...].astype(F32)
    rows = []
    for c in range(4):
        rows += [k1_scratch[:, c, :], jnp.zeros((5, 16), F32)]
    k1 = jnp.concatenate(rows, axis=0).astype(BF16)
    for ry in range(4):
        w1_ref[16 * ry : 16 * ry + 16, :] = dot(k1, chosen_ref[ry], ((0,), (0,))).astype(BF16)
    blank = jnp.zeros((16, 32), BF16)
    for kx in range(3):
        for kz in range(3):
            k = [k2_ref[9 * kx + 3 * ky + kz] for ky in range(3)]
            left = jnp.concatenate([k[1], k[2], blank, blank, k[0]], axis=0)
            right = jnp.concatenate([blank, k[0], k[1], k[2], blank], axis=0)
            base = ROWS1 * (3 * kx + kz)
            w2_ref[base : base + ROWS1, :] = jnp.concatenate([left, right], axis=1)
            base = ROWS2 * (3 * kx + kz)
            for at, ky in enumerate((1, 2, 0)):
                w3_ref[base + 32 * at : base + 32 * at + 32, :] = k3_ref[9 * kx + 3 * ky + kz]


def with_shifts(act, classes, first, ref, x):
    act = act.astype(BF16).astype(F32)
    for zc in range(classes):
        block = act[:, 128 * zc : 128 * zc + 128]
        block = jnp.concatenate([block, up_y(block[first:])], axis=0)
        size = block.shape[0]
        ref[x, size * (zc + 1) : size * (zc + 2), :] = block.astype(BF16)
        if zc == classes - 1:
            ref[x, 0:size, :] = up_z(block).astype(BF16)


def prepare(
    dens_hbm, halo_hbm, k1_hbm, k2_hbm, k3_hbm, chosen_hbm,
    planes_ref, w1_ref, w2_ref, w3_ref,
    dens_ref, halo_ref, k1_ref, k2_ref, k3_ref, chosen_ref, sems, perm_ref, wide_ref, k1_scratch,
):
    sources = (dens_hbm, halo_hbm, k1_hbm, k2_hbm, k3_hbm, chosen_hbm)
    targets = (dens_ref, halo_ref, k1_ref, k2_ref, k3_ref, chosen_ref)
    copies = [pltpu.make_async_copy(a, b, sems.at[i]) for i, (a, b) in enumerate(zip(sources, targets))]
    for copy in copies:
        copy.start()
    wide_ref[ABOVE : ABOVE + 64, 0:128] = jnp.zeros((64, CELLS), F32)
    wide_ref[ABOVE + 56 : ABOVE + 64, 128:1024] = jnp.zeros((8, 896), F32)
    fill_permutation(perm_ref)
    for copy in copies:
        copy.wait()
    for x in range(8):
        spread_plane(dens_ref.at[:, x], wide_ref, OWN + 32 * x, 7 + x)
    for x in range(7):
        spread_plane(halo_ref.at[:, 1 + x], wide_ref, HALO + 32 * x, x)
    to_cells(wide_ref, perm_ref, OWN, ABOVE + 64, [*range(7, 15), *range(7)], True, planes_ref)
    arrange_kernels(k1_ref, k2_ref, k3_ref, chosen_ref, k1_scratch, w1_ref, w2_ref, w3_ref)


def layers(
    planes_ref, w1_ref, w2_ref, w3_ref, cot_ref, chosen_hbm,
    message_ref,
    chosen_ref, sem, cols1_ref, slope1_ref, act1_ref, cols2_ref, slope2_ref, act2_ref, up2_ref, up1_ref, delta1_ref,
    whole_ref,
):
    copy = pltpu.make_async_copy(chosen_hbm, chosen_ref, sem)
    copy.start()
    w1 = w1_ref[...]
    for rx in range(7):
        for kx in range(3):
            for rz in range(4):
                lanes = slice(512 * rx + 128 * rz, 512 * rx + 128 * rz + 128)
                part = planes_ref[2 * rx + kx, 96 * rz : 96 * rz + 144, :]
                cols1_ref[144 * kx : 144 * kx + 144, lanes] = part
        lanes = slice(512 * rx, 512 * rx + 512)
        act, slope1_ref[:, lanes] = gelu_and_slope(dot(w1, cols1_ref[:, lanes], ((1,), (0,))))
        with_shifts(act, 4, 48, act1_ref, rx)
    for rx in range(3):
        for kx in range(3):
            for rz in range(2):
                part = act1_ref[2 * rx + kx, 160 * rz : 160 * rz + 240, :]
                lanes = slice(128 * (2 * rx + rz), 128 * (2 * rx + rz) + 128)
                cols2_ref[240 * kx : 240 * kx + 240, lanes] = part
    act, slope2_ref[...] = gelu_and_slope(dot(w2_ref[...], cols2_ref[...], ((0,), (0,))))
    for rx in range(3):
        with_shifts(act[:, 256 * rx : 256 * rx + 256], 2, 32, act2_ref, rx)
    cols3 = act2_ref[...].reshape(9 * ROWS2, CELLS)
    feat, slope3 = gelu_and_slope(dot(w3_ref[...], cols3, ((0,), (0,))))
    feat = feat.astype(BF16).astype(F32)

    delta3 = (cot_ref[:, 0, :] * slope3).astype(BF16)
    third = jnp.concatenate([dot(delta3, cols3, ((1,), (1,))), jnp.zeros((64, 32), F32)], axis=1)
    up2_ref[...] = dot(w3_ref[...], delta3, ((1,), (0,)))

    def folded2(kx, kz):
        base = ROWS2 * (3 * kx + kz)
        block = up2_ref[base : base + 64, :]
        return jnp.concatenate([block[:32], block[32:] + down_y(up2_ref[base + 64 : base + 96, :])], axis=0)

    delta2 = []
    for kx in range(3):
        for part in (folded2(kx, 1), folded2(kx, 2) + down_z(folded2(kx, 0))):
            at = 128 * len(delta2)
            delta2.append((part * slope2_ref[:, at : at + 128]).astype(BF16))
    delta2 = jnp.concatenate(delta2, axis=1)
    whole2 = dot(delta2, cols2_ref[...], ((1,), (1,)))
    pieces = [None] * 27
    for kx in range(3):
        for kz in range(3):
            base = ROWS1 * (3 * kx + kz)
            for ky in range(3):
                at0 = base + 16 * ((ky - 1) % 5)
                at1 = base + 16 * (ky + 1)
                pieces[9 * kx + 3 * ky + kz] = whole2[:32, at0 : at0 + 16] + whole2[32:, at1 : at1 + 16]
    second = jnp.concatenate(pieces + [jnp.zeros((32, 80), F32)], axis=1)
    up1_ref[...] = dot(w2_ref[...], delta2, ((1,), (0,)))

    def folded1(x, kz, rz):
        total = None
        for kx in range(3):
            rx = x - kx
            if rx % 2 == 0 and 0 <= rx // 2 < 3:
                base = ROWS1 * (3 * kx + kz)
                lanes = slice(128 * (rx + rz), 128 * (rx + rz) + 128)
                part = up1_ref[base : base + ROWS1, lanes]
                total = part if total is None else total + part
        return total

    for x in range(7):
        for zc in range(4):
            if zc % 2 == 0:
                block = folded1(x, 1, zc // 2)
            elif zc == 1:
                block = folded1(x, 2, 0) + folded1(x, 0, 1)
            else:
                block = folded1(x, 2, 1) + down_z(folded1(x, 0, 0))
            block = jnp.concatenate([block[:48], block[48:64] + down_y(block[64:])], axis=0)
            lanes = slice(512 * x + 128 * zc, 512 * x + 128 * zc + 128)
            delta1_ref[:, lanes] = (block * slope1_ref[:, lanes]).astype(BF16)
    whole1 = dot(delta1_ref[...], cols1_ref[...], ((1,), (1,)))
    parts = []
    for _ in range(3):
        parts.append(whole1.astype(BF16))
        whole1 = whole1 - parts[-1].astype(F32)
    first = None
    copy.wait()
    for ry in range(4):
        rows = jnp.concatenate([part[16 * ry : 16 * ry + 16] for part in parts], axis=0)
        got = dot(rows, chosen_ref[ry], ((1,), (1,)))
        for at in (0, 16, 32):
            first = got[at : at + 16] if first is None else first + got[at : at + 16]

    def put(row, value):
        whole_ref[pl.ds(row, 16, stride=48), :] = value

    for x in range(4):
        for r in range(7):
            put(8 * x + r, third[16 * x : 16 * x + 16, 128 * r : 128 * r + 128])
        put(8 * x + 7, feat[16 * x : 16 * x + 16])
    for h in range(2):
        for r in range(4):
            value = second[16 * h : 16 * h + 16, 128 * r : 128 * r + 128]
            if r == 3:
                value = jnp.where(lane_iota(16) < 64, value, pltpu.roll(first, 64, 1) if h == 0 else first)
            upper = value.astype(BF16).astype(F32)
            put(32 + 4 * h + r, upper)
            put(40 + 4 * h + r, value - upper)
    message_ref[...] = whole_ref[...].astype(BF16)


def passed_along(block, axis, distance):
    devices = range(lax.axis_size(axis))
    route = [(i, i + distance) for i in devices if i + distance in devices]
    return lax.ppermute(block, axis, route)


def turn(cot_hbm, out_ref, cot_ref, sem):
    copy = pltpu.make_async_copy(cot_hbm, cot_ref, sem)
    copy.start()
    copy.wait()
    out_ref[:, 0, :] = cot_ref[...].astype(F32).T


def regroup(got_ref, message_ref, whole_ref):
    whole_ref[...] = got_ref[...].astype(F32)
    total = whole_ref[0:48, :]
    for j in range(1, 16):
        total = total + whole_ref[48 * j : 48 * j + 48, :]
    shared = total[32:40] + total[40:48]
    for x in range(4):
        sums = jnp.concatenate([total[8 * x : 8 * x + 8], shared], axis=0).astype(BF16)
        feat = whole_ref[pl.ds(8 * x + 7, 16, stride=48), :].astype(BF16)
        for dp in range(4):
            base = 128 * dp + 32 * x
            message_ref[base : base + 16, :] = sums
            message_ref[base + 16 : base + 32, :] = feat


def total_of(got_ref):
    total = got_ref[0:16, :].astype(F32)
    for j in range(1, 16):
        total = total + got_ref[32 * j : 32 * j + 16, :].astype(F32)
    return total


def share(got_ref, message_ref):
    total = total_of(got_ref)[8:]
    for j in range(16):
        message_ref[8 * j : 8 * j + 8, :] = total


def settle(dp_ref, got_ref, feat_ref, third_ref):
    base = pl.multiple_of(128 * dp_ref[0], 128)
    feat = [got_ref[pl.ds(base + 32 * x + 16, 16), :].astype(F32) for x in range(4)]
    feat_ref[...] = jnp.concatenate(feat, axis=0).T.astype(BF16)
    total = total_of(got_ref)[:8]
    turned = [total] + [pltpu.roll(total, 128 - 32 * q, 1) for q in range(1, 4)]
    for kx in range(3):
        for kz in range(3):
            for at, ky in enumerate((1, 2, 0)):
                b = 9 * kx + 3 * kz + at
                third_ref[9 * kx + 3 * ky + kz] = turned[b % 4][b // 4 : b // 4 + 1, :32]


def unpack(got_ref, first_ref, second_ref):
    halves = []
    for h in range(2):
        halves.append(jnp.concatenate([got_ref[pl.ds(4 * h + r, 16, stride=8), :] for r in range(4)], axis=1))
    both = jnp.concatenate(halves, axis=0).T
    second_ref[...] = both[:432]
    for c in range(4):
        h, q = c // 2, c % 2
        first_ref[:, c, :] = both[448 + 32 * q : 475 + 32 * q, 16 * h : 16 * h + 16]


def vmem(*shape, dtype=F32):
    return pltpu.VMEM(shape, dtype)


def call(kernel, out_shape, scratch=(), limit=8, **options):
    return pl.pallas_call(
        kernel,
        out_shape=out_shape,
        scratch_shapes=list(scratch),
        compiler_params=pltpu.CompilerParams(vmem_limit_bytes=limit * 1024 * 1024),
        **options,
    )


IN_HBM = pl.BlockSpec(memory_space=pltpu.HBM)
IN_VMEM = pl.BlockSpec(memory_space=pltpu.VMEM)


def in_hbm(array):
    return pltpu.with_memory_space_constraint(array, pltpu.HBM)


def in_vmem(array):
    return pltpu.with_memory_space_constraint(array, pltpu.VMEM)


def local_message(halo, dens, k1, k2, k3, cot):
    chosen = jnp.asarray(first_selection(), BF16)
    k1 = jnp.transpose(k1, (2, 3, 4, 1, 0)).reshape(27, 4, 16)
    k2 = jnp.transpose(k2, (2, 3, 4, 1, 0)).reshape(27, 16, 32)
    k3 = jnp.transpose(k3, (2, 3, 4, 1, 0)).reshape(27, 32, 64)
    arguments = (dens, halo, k1, k2, k3, chosen)
    pinned = [array if array is halo else in_hbm(array) for array in arguments]
    prepared = call(
        prepare,
        (
            vmem(15, 9 * ROWS0, CELLS, dtype=BF16),
            vmem(64, 9 * ROWS0, dtype=BF16),
            vmem(9 * ROWS1, 64, dtype=BF16),
            vmem(9 * ROWS2, 64, dtype=BF16),
        ),
        [
            *(vmem(*array.shape, dtype=BF16) for array in arguments),
            pltpu.SemaphoreType.DMA((6,)),
            vmem(1024, 1152, dtype=BF16),
            vmem(ABOVE + 64, 1024),
            vmem(27, 4, 16),
        ],
        20,
        in_specs=[IN_HBM, pl.BlockSpec(memory_space=pl.ANY)] + [IN_HBM] * 4,
        out_specs=(IN_VMEM,) * 4,
    )(*pinned)
    return call(
        layers,
        jax.ShapeDtypeStruct((768, CELLS), BF16),
        [
            vmem(*chosen.shape, dtype=BF16),
            pltpu.SemaphoreType.DMA,
            vmem(9 * ROWS0, 3584, dtype=BF16),
            vmem(64, 3584),
            vmem(7, 5 * ROWS1, CELLS, dtype=BF16),
            vmem(9 * ROWS1, 768, dtype=BF16),
            vmem(64, 768),
            vmem(3, 3 * ROWS2, CELLS, dtype=BF16),
            vmem(9 * ROWS2, CELLS),
            vmem(9 * ROWS1, 768),
            vmem(64, 3584, dtype=BF16),
            vmem(768, CELLS),
        ],
        26,
        in_specs=[IN_VMEM] * 5 + [IN_HBM],
    )(*map(in_vmem, prepared), cot, in_hbm(chosen))


def exchanged(rows, axes):
    size = lax.axis_size(axes)
    blocks = rows.reshape(size, rows.shape[0] // size, CELLS)
    return lax.all_to_all(blocks, axes, 0, 0, tiled=True).reshape(rows.shape)


def shards(density_cubes, first_kernel, second_kernel, third_kernel, cotangent):
    shape = jax.ShapeDtypeStruct
    dens = density_cubes[0]
    halo = passed_along(dens, SPACE, 1)
    cot = jnp.transpose(cotangent, (0, 1, 3, 4, 2)).reshape(CELLS, 64)
    scratch = [vmem(CELLS, 64, dtype=BF16), pltpu.SemaphoreType.DMA]
    cot = call(turn, shape((64, 1, CELLS), F32), scratch, in_specs=[IN_HBM])(in_hbm(cot))
    cot = lax.all_to_all(cot, SPACE, 0, 0, tiled=True)
    message = local_message(halo, dens, first_kernel, second_kernel, third_kernel, cot)
    got = exchanged(message, NEAR)
    got = exchanged(call(regroup, shape((512, CELLS), BF16), [vmem(768, CELLS)])(got), FAR)
    both = exchanged(call(share, shape((CELLS, CELLS), F32))(got), NEAR)
    specs = [pl.BlockSpec(memory_space=pltpu.SMEM), pl.BlockSpec()]
    dp = lax.axis_index("dp").reshape(1)
    feat, third = call(settle, (shape((CELLS, 64), BF16), shape((27, 1, 32), F32)), in_specs=specs)(dp, got)
    first, second = call(unpack, (shape((27, 4, 16), F32), shape((432, 32), F32)))(both)
    features = jnp.transpose(feat.reshape(1, 1, 8, 16, 64), (0, 1, 4, 2, 3))
    first_grad = jnp.transpose(first.reshape(3, 3, 3, 4, 16), (4, 3, 0, 1, 2))
    second_grad = jnp.transpose(second.reshape(3, 3, 3, 16, 32), (4, 3, 0, 1, 2))
    third_grad = jnp.transpose(third.reshape(3, 3, 3, 1, 32), (3, 4, 0, 1, 2))
    return (features, first_grad, second_grad, third_grad)


def solution(mesh):
    mesh = jax.sharding.Mesh(mesh.devices.reshape(4, 4, 2, 4, 2), ("dp",) + SPACE)
    in_specs = (
        P("dp", None, SPACE, None, None),
        P(),
        P(),
        P(),
        P("dp", SPACE, None, None, None),
    )
    out_specs = (P("dp", SPACE, None, None, None), P(), P(), P(SPACE, None, None, None, None))
    return jax.shard_map(shards, mesh=mesh, in_specs=in_specs, out_specs=out_specs, check_vma=False)
```

```python
import math

import jax
import jax.numpy as jnp
import numpy as np
from jax import lax
from jax.experimental import pallas as pl
from jax.experimental.pallas import tpu as pltpu
from jax.sharding import PartitionSpec as P


BF16 = jnp.bfloat16
F32 = jnp.float32
CELLS = 128
ROWS0, ROWS1, ROWS2 = 48, 80, 96
SCALE = math.sqrt(2.0 / math.pi)
SPACE = ("x", "z", "y", "core")
NEAR = ("z", "y", "core")
FAR = ("dp", "x")


def first_selection():
    chosen = np.zeros((4, 4, 32, 9, ROWS0), np.float32)
    for ry in range(4):
        for c in range(4):
            for kx in range(3):
                for ky in range(3):
                    for kz in range(3):
                        y = 2 * ry + ky - 1
                        row = 32 + c if y < 0 else 8 * c + y
                        chosen[ry, c, 9 * kx + 3 * ky + kz, 3 * kx + kz, row] = 1
    return chosen.reshape(4, 128, 9 * ROWS0)


def dot(a, b, contract, precision=None):
    return lax.dot_general(a, b, (contract, ((), ())), preferred_element_type=F32, precision=precision)


def lane_iota(rows):
    return lax.broadcasted_iota(jnp.int32, (rows, CELLS), 1)


def up_y(block):
    return jnp.where(lane_iota(block.shape[0]) >= 16, pltpu.roll(block, 16, 1), 0.0)


def up_z(block):
    return jnp.where(lane_iota(block.shape[0]) % 16 != 0, pltpu.roll(block, 1, 1), 0.0)


def down_y(block):
    return jnp.where(lane_iota(block.shape[0]) < CELLS - 16, pltpu.roll(block, CELLS - 16, 1), 0.0)


def down_z(block):
    return jnp.where(lane_iota(block.shape[0]) % 16 != 15, pltpu.roll(block, CELLS - 1, 1), 0.0)


def gelu_and_slope(x):
    square = x * x
    t = jnp.tanh(SCALE * (x + 0.044715 * (x * square)))
    half = 0.5 * (1.0 + t)
    slope = half + 0.5 * x * (1.0 - t * t) * (SCALE * (1.0 + 3 * 0.044715 * square))
    return x * half, slope


def fill_permutation(perm_ref):
    z = lax.broadcasted_iota(jnp.int32, (CELLS, CELLS), 0)
    u = lane_iota(CELLS)
    offset = z - 8 * (u % 16)
    for zi in range(9):
        hit = offset == zi - 1
        for y in range(8):
            block = jnp.where(hit & (u // 16 == y), 1.0, 0.0)
            perm_ref[128 * y : 128 * y + 128, 128 * zi : 128 * zi + 128] = block.astype(BF16)


OWN, HALO, ABOVE = 0, 256, 480


def spread_plane(plane_ref, wide_ref, base, x):
    for c in range(4):
        plane = plane_ref[c].astype(F32)
        for y in range(8):
            tile = plane[8 * y : 8 * y + 8]
            wide_ref[base + 8 * c : base + 8 * c + 8, 128 * y : 128 * y + 128] = tile
            if y < 7:
                row = ABOVE + 4 * x + c
                wide_ref[row : row + 1, 128 * y + 128 : 128 * y + 256] = tile[7:8]


def to_cells(wide_ref, perm_ref, start, stop, planes, above, out_ref):
    rows = wide_ref[start:stop, :].astype(BF16)
    upper = lax.broadcasted_iota(jnp.int32, (8, CELLS), 0) < 4
    for first in range(0, 9, 2):
        count = min(2, 9 - first)
        got = dot(rows, perm_ref[:, 128 * first : 128 * (first + count)], ((1,), (0,)))
        for j in range(count):
            lanes = slice(128 * j, 128 * j + 128)
            base = ROWS0 * (first + j)
            for at, x in enumerate(planes):
                out_ref[x, base : base + 32, :] = got[32 * at : 32 * at + 32, lanes].astype(BF16)
            if above:
                for x in range(15):
                    at = 32 * len(planes) + 8 * (x // 2)
                    tile = got[at : at + 8, lanes]
                    tile = jnp.where(upper, tile if x % 2 == 0 else pltpu.roll(tile, 4, 0), 0.0)
                    tile = jnp.concatenate([tile, jnp.zeros((8, CELLS), F32)], axis=0)
                    out_ref[x, base + 32 : base + 48, :] = tile.astype(BF16)


def arrange_kernels(k1_ref, k2_ref, k3_ref, chosen_ref, k1_scratch, w1_ref, w2_ref, w3_ref, w2t_ref, w3t_ref):
    k1_scratch[...] = k1_ref[...].astype(F32)
    rows = []
    for c in range(4):
        rows += [k1_scratch[:, c, :], jnp.zeros((5, 16), F32)]
    k1 = jnp.concatenate(rows, axis=0).astype(BF16)
    for ry in range(4):
        w1_ref[16 * ry : 16 * ry + 16, :] = dot(k1, chosen_ref[ry], ((0,), (0,))).astype(BF16)
    blank = jnp.zeros((16, 32), BF16)
    for kx in range(3):
        for kz in range(3):
            k = [k2_ref[9 * kx + 3 * ky + kz] for ky in range(3)]
            left = jnp.concatenate([k[1], k[2], blank, blank, k[0]], axis=0)
            right = jnp.concatenate([blank, k[0], k[1], k[2], blank], axis=0)
            base = ROWS1 * (3 * kx + kz)
            w2_ref[base : base + ROWS1, :] = jnp.concatenate([left, right], axis=1)
            base = ROWS2 * (3 * kx + kz)
            for at, ky in enumerate((1, 2, 0)):
                w3_ref[base + 32 * at : base + 32 * at + 32, :] = k3_ref[9 * kx + 3 * ky + kz]
    w2t_ref[...] = w2_ref[...].astype(F32).T.astype(BF16)
    w3t_ref[...] = w3_ref[...].astype(F32).T.astype(BF16)


def with_shifts(act, classes, first, ref, x):
    act = act.astype(BF16).astype(F32)
    for zc in range(classes):
        block = act[:, 128 * zc : 128 * zc + 128]
        block = jnp.concatenate([block, up_y(block[first:])], axis=0)
        size = block.shape[0]
        ref[x, size * (zc + 1) : size * (zc + 2), :] = block.astype(BF16)
        if zc == classes - 1:
            ref[x, 0:size, :] = up_z(block).astype(BF16)


def prepare(
    dens_ref, halo_any, k1_hbm, k2_hbm, k3_hbm, chosen_hbm,
    planes_ref, w1_ref, w2_ref, w3_ref, w2t_ref, w3t_ref,
    halo_ref, k1_ref, k2_ref, k3_ref, chosen_ref, sems, perm_ref, wide_ref, k1_scratch,
):
    sources = (halo_any, k1_hbm, k2_hbm, k3_hbm, chosen_hbm)
    targets = (halo_ref, k1_ref, k2_ref, k3_ref, chosen_ref)
    copies = [pltpu.make_async_copy(a, b, sems.at[i]) for i, (a, b) in enumerate(zip(sources, targets))]
    for copy in copies:
        copy.start()
    wide_ref[ABOVE : ABOVE + 64, 0:128] = jnp.zeros((64, CELLS), F32)
    wide_ref[ABOVE + 56 : ABOVE + 64, 128:1024] = jnp.zeros((8, 896), F32)
    fill_permutation(perm_ref)
    for x in range(8):
        spread_plane(dens_ref.at[:, x], wide_ref, OWN + 32 * x, 7 + x)
    copies[0].wait()
    for x in range(7):
        spread_plane(halo_ref.at[:, 1 + x], wide_ref, HALO + 32 * x, x)
    to_cells(wide_ref, perm_ref, OWN, ABOVE + 64, [*range(7, 15), *range(7)], True, planes_ref)
    for copy in copies[1:]:
        copy.wait()
    arrange_kernels(k1_ref, k2_ref, k3_ref, chosen_ref, k1_scratch, w1_ref, w2_ref, w3_ref, w2t_ref, w3t_ref)


def layers(
    planes_ref, w1_ref, w2_ref, w3_ref, w2t_ref, w3t_ref, cot_ref, chosen_hbm,
    message_ref,
    chosen_ref, sem, cols1_ref, slope1_ref, act1_ref, cols2_ref, slope2_ref, act2_ref, up2_ref, up1_ref, delta1_ref,
    whole_ref,
):
    copy = pltpu.make_async_copy(chosen_hbm, chosen_ref, sem)
    copy.start()
    w1 = w1_ref[...]
    for rx in range(7):
        for kx in range(3):
            for rz in range(4):
                lanes = slice(512 * rx + 128 * rz, 512 * rx + 128 * rz + 128)
                part = planes_ref[2 * rx + kx, 96 * rz : 96 * rz + 144, :]
                cols1_ref[144 * kx : 144 * kx + 144, lanes] = part
        lanes = slice(512 * rx, 512 * rx + 512)
        act, slope1_ref[:, lanes] = gelu_and_slope(dot(w1, cols1_ref[:, lanes], ((1,), (0,))))
        with_shifts(act, 4, 48, act1_ref, rx)
    for rx in range(3):
        for kx in range(3):
            for rz in range(2):
                part = act1_ref[2 * rx + kx, 160 * rz : 160 * rz + 240, :]
                lanes = slice(128 * (2 * rx + rz), 128 * (2 * rx + rz) + 128)
                cols2_ref[240 * kx : 240 * kx + 240, lanes] = part
    act, slope2_ref[...] = gelu_and_slope(dot(w2t_ref[...], cols2_ref[...], ((1,), (0,))))
    for rx in range(3):
        with_shifts(act[:, 256 * rx : 256 * rx + 256], 2, 32, act2_ref, rx)
    cols3 = act2_ref[...].reshape(9 * ROWS2, CELLS)
    feat, slope3 = gelu_and_slope(dot(w3t_ref[...], cols3, ((1,), (0,))))
    feat = feat.astype(BF16).astype(F32)

    delta3 = (cot_ref[:, 0, :] * slope3).astype(BF16)
    third = jnp.concatenate([dot(delta3, cols3, ((1,), (1,))), jnp.zeros((64, 32), F32)], axis=1)
    up2_ref[...] = dot(w3_ref[...], delta3, ((1,), (0,)))

    def folded2(kx, kz):
        base = ROWS2 * (3 * kx + kz)
        block = up2_ref[base : base + 64, :]
        return jnp.concatenate([block[:32], block[32:] + down_y(up2_ref[base + 64 : base + 96, :])], axis=0)

    delta2 = []
    for kx in range(3):
        for part in (folded2(kx, 1), folded2(kx, 2) + down_z(folded2(kx, 0))):
            at = 128 * len(delta2)
            delta2.append((part * slope2_ref[:, at : at + 128]).astype(BF16))
    delta2 = jnp.concatenate(delta2, axis=1)
    whole2 = [dot(cols2_ref[...], delta2[32 * ry : 32 * ry + 32], ((1,), (1,))) for ry in range(2)]
    pieces = []
    for kx in range(3):
        for ky in range(3):
            for kz in range(3):
                base = ROWS1 * (3 * kx + kz)
                at0 = base + 16 * ((ky - 1) % 5)
                at1 = base + 16 * (ky + 1)
                pieces.append(whole2[0][at0 : at0 + 16] + whole2[1][at1 : at1 + 16])
    second = jnp.concatenate(pieces + [jnp.zeros((80, 32), F32)], axis=0).T
    up1_ref[...] = dot(w2_ref[...], delta2, ((1,), (0,)))

    def folded1(x, kz, rz):
        total = None
        for kx in range(3):
            rx = x - kx
            if rx % 2 == 0 and 0 <= rx // 2 < 3:
                base = ROWS1 * (3 * kx + kz)
                lanes = slice(128 * (rx + rz), 128 * (rx + rz) + 128)
                part = up1_ref[base : base + ROWS1, lanes]
                total = part if total is None else total + part
        return total

    for x in range(7):
        for zc in range(4):
            if zc % 2 == 0:
                block = folded1(x, 1, zc // 2)
            elif zc == 1:
                block = folded1(x, 2, 0) + folded1(x, 0, 1)
            else:
                block = folded1(x, 2, 1) + down_z(folded1(x, 0, 0))
            block = jnp.concatenate([block[:48], block[48:64] + down_y(block[64:])], axis=0)
            lanes = slice(512 * x + 128 * zc, 512 * x + 128 * zc + 128)
            delta1_ref[:, lanes] = (block * slope1_ref[:, lanes]).astype(BF16)
    whole1 = dot(delta1_ref[...], cols1_ref[...], ((1,), (1,)))
    parts = []
    for _ in range(3):
        parts.append(whole1.astype(BF16))
        whole1 = whole1 - parts[-1].astype(F32)
    first = None
    copy.wait()
    for ry in range(4):
        rows = jnp.concatenate([part[16 * ry : 16 * ry + 16] for part in parts], axis=0)
        got = dot(rows, chosen_ref[ry], ((1,), (1,)))
        for at in (0, 16, 32):
            first = got[at : at + 16] if first is None else first + got[at : at + 16]

    def put(row, value):
        whole_ref[pl.ds(row, 16, stride=48), :] = value

    for x in range(4):
        for r in range(7):
            put(8 * x + r, third[16 * x : 16 * x + 16, 128 * r : 128 * r + 128])
        put(8 * x + 7, feat[16 * x : 16 * x + 16])
    for h in range(2):
        for r in range(4):
            value = second[16 * h : 16 * h + 16, 128 * r : 128 * r + 128]
            if r == 3:
                value = jnp.where(lane_iota(16) < 64, value, pltpu.roll(first, 64, 1) if h == 0 else first)
            upper = value.astype(BF16).astype(F32)
            put(32 + 4 * h + r, upper)
            put(40 + 4 * h + r, value - upper)
    message_ref[...] = whole_ref[0:768, :].astype(BF16)


def passed_along(block, axis, distance):
    devices = range(lax.axis_size(axis))
    route = [(i, i + distance) for i in devices if i + distance in devices]
    return lax.ppermute(block, axis, route)


def fetch(cot_hbm, dens_hbm, out_ref, dens_ref, cot_ref, sems):
    copies = [pltpu.make_async_copy(cot_hbm, cot_ref, sems.at[0]), pltpu.make_async_copy(dens_hbm, dens_ref, sems.at[1])]
    for copy in copies:
        copy.start()
    copies[0].wait()
    out_ref[:, 0, :] = cot_ref[...].astype(F32).T
    copies[1].wait()


def regroup(got_ref, message_ref, whole_ref):
    whole_ref[0:768, :] = got_ref[...].astype(F32)
    total = whole_ref[0:48, :]
    for j in range(1, 16):
        total = total + whole_ref[48 * j : 48 * j + 48, :]
    shared = total[32:40] + total[40:48]
    for x in range(4):
        sums = jnp.concatenate([total[8 * x : 8 * x + 8], shared], axis=0).astype(BF16)
        feat = whole_ref[pl.ds(8 * x + 7, 16, stride=48), :].astype(BF16)
        for dp in range(4):
            base = 128 * dp + 32 * x
            message_ref[base : base + 16, :] = sums
            message_ref[base + 16 : base + 32, :] = feat


def total_of(got_ref):
    total = got_ref[0:16, :].astype(F32)
    for j in range(1, 16):
        total = total + got_ref[32 * j : 32 * j + 16, :].astype(F32)
    return total


def share(got_ref, message_ref):
    total = total_of(got_ref)[8:]
    for j in range(16):
        message_ref[8 * j : 8 * j + 8, :] = total


def finish(dp_ref, got_ref, shared_ref, feat_ref, first_ref, second_ref, third_ref, whole_ref):
    whole_ref[0:CELLS, :] = shared_ref[...]
    base = pl.multiple_of(128 * dp_ref[0], 128)
    feat = [got_ref[pl.ds(base + 32 * x + 16, 16), :].astype(F32) for x in range(4)]
    feat_ref[...] = jnp.concatenate(feat, axis=0).T.astype(BF16)
    total = total_of(got_ref)[:8]
    turned = [total] + [pltpu.roll(total, 128 - 32 * q, 1) for q in range(1, 4)]
    for kx in range(3):
        for kz in range(3):
            for at, ky in enumerate((1, 2, 0)):
                b = 9 * kx + 3 * kz + at
                third_ref[9 * kx + 3 * ky + kz] = turned[b % 4][b // 4 : b // 4 + 1, :32]
    halves = []
    for h in range(2):
        halves.append(jnp.concatenate([whole_ref[pl.ds(4 * h + r, 16, stride=8), :] for r in range(4)], axis=1))
    both = jnp.concatenate(halves, axis=0).T
    second_ref[...] = both[:432]
    for c in range(4):
        h, q = c // 2, c % 2
        first_ref[:, c, :] = both[448 + 32 * q : 475 + 32 * q, 16 * h : 16 * h + 16]


def vmem(*shape, dtype=F32):
    return pltpu.VMEM(shape, dtype)


def call(kernel, out_shape, scratch=(), limit=8, **options):
    return pl.pallas_call(
        kernel,
        out_shape=out_shape,
        scratch_shapes=list(scratch),
        compiler_params=pltpu.CompilerParams(vmem_limit_bytes=limit * 1024 * 1024),
        **options,
    )


IN_HBM = pl.BlockSpec(memory_space=pltpu.HBM)
IN_VMEM = pl.BlockSpec(memory_space=pltpu.VMEM)


def in_hbm(array):
    return pltpu.with_memory_space_constraint(array, pltpu.HBM)


def in_vmem(array):
    return pltpu.with_memory_space_constraint(array, pltpu.VMEM)


def fetched(cot, dens):
    return call(
        fetch,
        (jax.ShapeDtypeStruct((64, 1, CELLS), F32), vmem(*dens.shape, dtype=BF16)),
        [vmem(CELLS, 64, dtype=BF16), pltpu.SemaphoreType.DMA((2,))],
        in_specs=[IN_HBM] * 2,
        out_specs=(IN_VMEM,) * 2,
    )(in_hbm(cot), in_hbm(dens))


def local_message(halo, dens, k1, k2, k3, cot):
    chosen = jnp.asarray(first_selection(), BF16)
    k1 = jnp.transpose(k1, (2, 3, 4, 1, 0)).reshape(27, 4, 16)
    k2 = jnp.transpose(k2, (2, 3, 4, 1, 0)).reshape(27, 16, 32)
    k3 = jnp.transpose(k3, (2, 3, 4, 1, 0)).reshape(27, 32, 64)
    arguments = (halo, k1, k2, k3, chosen)
    prepared = call(
        prepare,
        (
            vmem(15, 9 * ROWS0, CELLS, dtype=BF16),
            vmem(64, 9 * ROWS0, dtype=BF16),
            vmem(9 * ROWS1, 64, dtype=BF16),
            vmem(9 * ROWS2, 64, dtype=BF16),
            vmem(64, 9 * ROWS1, dtype=BF16),
            vmem(64, 9 * ROWS2, dtype=BF16),
        ),
        [
            *(vmem(*array.shape, dtype=BF16) for array in arguments),
            pltpu.SemaphoreType.DMA((5,)),
            vmem(1024, 1152, dtype=BF16),
            vmem(ABOVE + 64, 1024),
            vmem(27, 4, 16),
        ],
        20,
        in_specs=[IN_VMEM, pl.BlockSpec(memory_space=pl.ANY)] + [IN_HBM] * 4,
        out_specs=(IN_VMEM,) * 6,
    )(in_vmem(dens), halo, *map(in_hbm, arguments[1:]))
    return call(
        layers,
        jax.ShapeDtypeStruct((768, CELLS), BF16),
        [
            vmem(*chosen.shape, dtype=BF16),
            pltpu.SemaphoreType.DMA,
            vmem(9 * ROWS0, 3584, dtype=BF16),
            vmem(64, 3584),
            vmem(7, 5 * ROWS1, CELLS, dtype=BF16),
            vmem(9 * ROWS1, 768, dtype=BF16),
            vmem(64, 768),
            vmem(3, 3 * ROWS2, CELLS, dtype=BF16),
            vmem(9 * ROWS2, CELLS),
            vmem(9 * ROWS1, 768),
            vmem(64, 3584, dtype=BF16),
            vmem(816, CELLS),
        ],
        26,
        in_specs=[IN_VMEM] * 7 + [IN_HBM],
    )(*map(in_vmem, prepared), cot, in_hbm(chosen))


def exchanged(rows, axes):
    size = lax.axis_size(axes)
    blocks = rows.reshape(size, rows.shape[0] // size, CELLS)
    return lax.all_to_all(blocks, axes, 0, 0, tiled=True).reshape(rows.shape)


def shards(density_cubes, first_kernel, second_kernel, third_kernel, cotangent):
    shape = jax.ShapeDtypeStruct
    dens = density_cubes[0]
    halo = passed_along(dens, SPACE, 1)
    cot = jnp.transpose(cotangent, (0, 1, 3, 4, 2)).reshape(CELLS, 64)
    cot, dens = fetched(cot, dens)
    cot = lax.all_to_all(cot, SPACE, 0, 0, tiled=True)
    message = local_message(halo, dens, first_kernel, second_kernel, third_kernel, cot)
    message, dp = lax.optimization_barrier((message, lax.axis_index("dp").reshape(1)))
    got = exchanged(message, NEAR)
    got = exchanged(call(regroup, shape((512, CELLS), BF16), [vmem(816, CELLS)])(got), FAR)
    both = exchanged(call(share, shape((CELLS, CELLS), F32))(got), NEAR)
    outs = (shape((CELLS, 64), BF16), shape((27, 4, 16), F32), shape((432, 32), F32), shape((27, 1, 32), F32))
    specs = [pl.BlockSpec(memory_space=pltpu.SMEM), pl.BlockSpec(), pl.BlockSpec()]
    feat, first, second, third = call(finish, outs, [vmem(136, CELLS)], in_specs=specs)(dp, got, both)
    features = jnp.transpose(feat.reshape(1, 1, 8, 16, 64), (0, 1, 4, 2, 3))
    first_grad = jnp.transpose(first.reshape(3, 3, 3, 4, 16), (4, 3, 0, 1, 2))
    second_grad = jnp.transpose(second.reshape(3, 3, 3, 16, 32), (4, 3, 0, 1, 2))
    third_grad = jnp.transpose(third.reshape(3, 3, 3, 1, 32), (3, 4, 0, 1, 2))
    return (features, first_grad, second_grad, third_grad)


def solution(mesh):
    mesh = jax.sharding.Mesh(mesh.devices.reshape(4, 4, 2, 4, 2), ("dp",) + SPACE)
    in_specs = (
        P("dp", None, SPACE, None, None),
        P(),
        P(),
        P(),
        P("dp", SPACE, None, None, None),
    )
    out_specs = (P("dp", SPACE, None, None, None), P(), P(), P(SPACE, None, None, None, None))
    return jax.shard_map(shards, mesh=mesh, in_specs=in_specs, out_specs=out_specs, check_vma=False)
```

```python
import math

import jax
import jax.numpy as jnp
import numpy as np
from jax import lax
from jax.experimental import pallas as pl
from jax.experimental.pallas import tpu as pltpu
from jax.sharding import PartitionSpec as P


BF16 = jnp.bfloat16
F32 = jnp.float32
CELLS = 128
ROWS0, ROWS1, ROWS2 = 48, 80, 96
SCALE = math.sqrt(2.0 / math.pi)
SPACE = ("x", "z", "y", "core")
NEAR = ("z", "y", "core")
FAR = ("dp", "x")


def first_selection():
    chosen = np.zeros((4, 4, 32, 9, ROWS0), np.float32)
    for ry in range(4):
        for c in range(4):
            for kx in range(3):
                for ky in range(3):
                    for kz in range(3):
                        y = 2 * ry + ky - 1
                        row = 32 + c if y < 0 else 8 * c + y
                        chosen[ry, c, 9 * kx + 3 * ky + kz, 3 * kx + kz, row] = 1
    return chosen.reshape(4, 128, 9 * ROWS0)


def dot(a, b, contract, precision=None):
    return lax.dot_general(a, b, (contract, ((), ())), preferred_element_type=F32, precision=precision)


def lane_iota(rows):
    return lax.broadcasted_iota(jnp.int32, (rows, CELLS), 1)


def up_y(block):
    return jnp.where(lane_iota(block.shape[0]) >= 16, pltpu.roll(block, 16, 1), 0.0)


def up_z(block):
    return jnp.where(lane_iota(block.shape[0]) % 16 != 0, pltpu.roll(block, 1, 1), 0.0)


def down_y(block):
    return jnp.where(lane_iota(block.shape[0]) < CELLS - 16, pltpu.roll(block, CELLS - 16, 1), 0.0)


def down_z(block):
    return jnp.where(lane_iota(block.shape[0]) % 16 != 15, pltpu.roll(block, CELLS - 1, 1), 0.0)


def gelu_and_slope(x):
    square = x * x
    t = jnp.tanh(SCALE * (x + 0.044715 * (x * square)))
    half = 0.5 * (1.0 + t)
    slope = half + 0.5 * x * (1.0 - t * t) * (SCALE * (1.0 + 3 * 0.044715 * square))
    return x * half, slope


def fill_permutation(perm_ref):
    z = lax.broadcasted_iota(jnp.int32, (CELLS, CELLS), 0)
    u = lane_iota(CELLS)
    offset = z - 8 * (u % 16)
    for zi in range(9):
        hit = offset == zi - 1
        for y in range(8):
            block = jnp.where(hit & (u // 16 == y), 1.0, 0.0)
            perm_ref[128 * y : 128 * y + 128, 128 * zi : 128 * zi + 128] = block.astype(BF16)


OWN, HALO, ABOVE = 0, 256, 480


def spread_plane(plane_ref, wide_ref, base, x):
    for c in range(4):
        plane = plane_ref[c].astype(F32)
        for y in range(8):
            tile = plane[8 * y : 8 * y + 8]
            wide_ref[base + 8 * c : base + 8 * c + 8, 128 * y : 128 * y + 128] = tile
            if y < 7:
                row = ABOVE + 4 * x + c
                wide_ref[row : row + 1, 128 * y + 128 : 128 * y + 256] = tile[7:8]


def to_cells(wide_ref, perm_ref, start, stop, planes, above, out_ref):
    rows = wide_ref[start:stop, :].astype(BF16)
    upper = lax.broadcasted_iota(jnp.int32, (8, CELLS), 0) < 4
    for first in range(0, 9, 2):
        count = min(2, 9 - first)
        got = dot(rows, perm_ref[:, 128 * first : 128 * (first + count)], ((1,), (0,)))
        for j in range(count):
            lanes = slice(128 * j, 128 * j + 128)
            base = ROWS0 * (first + j)
            for at, x in enumerate(planes):
                out_ref[x, base : base + 32, :] = got[32 * at : 32 * at + 32, lanes].astype(BF16)
            if above:
                for x in range(15):
                    at = 32 * len(planes) + 8 * (x // 2)
                    tile = got[at : at + 8, lanes]
                    tile = jnp.where(upper, tile if x % 2 == 0 else pltpu.roll(tile, 4, 0), 0.0)
                    tile = jnp.concatenate([tile, jnp.zeros((8, CELLS), F32)], axis=0)
                    out_ref[x, base + 32 : base + 48, :] = tile.astype(BF16)


def arrange_kernels(k1_ref, k2_ref, k3_ref, chosen_ref, k1_scratch, w1_ref, w2_ref, w3_ref, w2t_ref, w3t_ref):
    k1_scratch[...] = k1_ref[...].astype(F32)
    rows = []
    for c in range(4):
        rows += [k1_scratch[:, c, :], jnp.zeros((5, 16), F32)]
    k1 = jnp.concatenate(rows, axis=0).astype(BF16)
    for ry in range(4):
        w1_ref[16 * ry : 16 * ry + 16, :] = dot(k1, chosen_ref[ry], ((0,), (0,))).astype(BF16)
    blank = jnp.zeros((16, 32), BF16)
    for kx in range(3):
        for kz in range(3):
            k = [k2_ref[9 * kx + 3 * ky + kz] for ky in range(3)]
            left = jnp.concatenate([k[1], k[2], blank, blank, k[0]], axis=0)
            right = jnp.concatenate([blank, k[0], k[1], k[2], blank], axis=0)
            base = ROWS1 * (3 * kx + kz)
            w2_ref[base : base + ROWS1, :] = jnp.concatenate([left, right], axis=1)
            base = ROWS2 * (3 * kx + kz)
            for at, ky in enumerate((1, 2, 0)):
                w3_ref[base + 32 * at : base + 32 * at + 32, :] = k3_ref[9 * kx + 3 * ky + kz]
    w2t_ref[...] = w2_ref[...].astype(F32).T.astype(BF16)
    w3t_ref[...] = w3_ref[...].astype(F32).T.astype(BF16)


def with_shifts(act, classes, first, ref, x):
    act = act.astype(BF16).astype(F32)
    for zc in range(classes):
        block = act[:, 128 * zc : 128 * zc + 128]
        block = jnp.concatenate([block, up_y(block[first:])], axis=0)
        size = block.shape[0]
        ref[x, size * (zc + 1) : size * (zc + 2), :] = block.astype(BF16)
        if zc == classes - 1:
            ref[x, 0:size, :] = up_z(block).astype(BF16)


def prepare(
    dens_ref, halo_any, k1_hbm, k2_hbm, k3_hbm, chosen_hbm,
    planes_ref, w1_ref, w2_ref, w3_ref, w2t_ref, w3t_ref,
    halo_ref, k1_ref, k2_ref, k3_ref, chosen_ref, sems, perm_ref, wide_ref, k1_scratch,
):
    sources = (halo_any, k1_hbm, k2_hbm, k3_hbm, chosen_hbm)
    targets = (halo_ref, k1_ref, k2_ref, k3_ref, chosen_ref)
    copies = [pltpu.make_async_copy(a, b, sems.at[i]) for i, (a, b) in enumerate(zip(sources, targets))]
    for copy in copies:
        copy.start()
    wide_ref[ABOVE : ABOVE + 64, 0:128] = jnp.zeros((64, CELLS), F32)
    wide_ref[ABOVE + 56 : ABOVE + 64, 128:1024] = jnp.zeros((8, 896), F32)
    fill_permutation(perm_ref)
    for x in range(8):
        spread_plane(dens_ref.at[:, x], wide_ref, OWN + 32 * x, 7 + x)
    copies[0].wait()
    for x in range(7):
        spread_plane(halo_ref.at[:, 1 + x], wide_ref, HALO + 32 * x, x)
    to_cells(wide_ref, perm_ref, OWN, ABOVE + 64, [*range(7, 15), *range(7)], True, planes_ref)
    for copy in copies[1:]:
        copy.wait()
    arrange_kernels(k1_ref, k2_ref, k3_ref, chosen_ref, k1_scratch, w1_ref, w2_ref, w3_ref, w2t_ref, w3t_ref)


def layers(
    planes_ref, w1_ref, w2_ref, w3_ref, w2t_ref, w3t_ref, cot_ref, chosen_hbm,
    message_ref,
    chosen_ref, sem, cols1_ref, slope1_ref, act1_ref, cols2_ref, slope2_ref, act2_ref, up2_ref, up1_ref, delta1_ref,
    whole_ref,
):
    copy = pltpu.make_async_copy(chosen_hbm, chosen_ref, sem)
    copy.start()
    w1 = w1_ref[...]
    for rx in range(7):
        for kx in range(3):
            for rz in range(4):
                lanes = slice(512 * rx + 128 * rz, 512 * rx + 128 * rz + 128)
                part = planes_ref[2 * rx + kx, 96 * rz : 96 * rz + 144, :]
                cols1_ref[144 * kx : 144 * kx + 144, lanes] = part
        lanes = slice(512 * rx, 512 * rx + 512)
        act, slope1_ref[:, lanes] = gelu_and_slope(dot(w1, cols1_ref[:, lanes], ((1,), (0,))))
        with_shifts(act, 4, 48, act1_ref, rx)
    for rx in range(3):
        for kx in range(3):
            for rz in range(2):
                part = act1_ref[2 * rx + kx, 160 * rz : 160 * rz + 240, :]
                lanes = slice(128 * (2 * rx + rz), 128 * (2 * rx + rz) + 128)
                cols2_ref[240 * kx : 240 * kx + 240, lanes] = part
    act, slope2_ref[...] = gelu_and_slope(dot(w2t_ref[...], cols2_ref[...], ((1,), (0,))))
    for rx in range(3):
        with_shifts(act[:, 256 * rx : 256 * rx + 256], 2, 32, act2_ref, rx)
    cols3 = act2_ref[...].reshape(9 * ROWS2, CELLS)
    feat, slope3 = gelu_and_slope(dot(w3t_ref[...], cols3, ((1,), (0,))))
    feat = feat.astype(BF16).astype(F32)

    delta3 = (cot_ref[:, 0, :] * slope3).astype(BF16)
    third = jnp.concatenate([dot(delta3, cols3, ((1,), (1,))), jnp.zeros((64, 32), F32)], axis=1)
    up2_ref[...] = dot(w3_ref[...], delta3, ((1,), (0,)))

    def folded2(kx, kz):
        base = ROWS2 * (3 * kx + kz)
        block = up2_ref[base : base + 64, :]
        return jnp.concatenate([block[:32], block[32:] + down_y(up2_ref[base + 64 : base + 96, :])], axis=0)

    delta2 = []
    for kx in range(3):
        for part in (folded2(kx, 1), folded2(kx, 2) + down_z(folded2(kx, 0))):
            at = 128 * len(delta2)
            delta2.append((part * slope2_ref[:, at : at + 128]).astype(BF16))
    delta2 = jnp.concatenate(delta2, axis=1)
    whole2 = [dot(cols2_ref[...], delta2[32 * ry : 32 * ry + 32], ((1,), (1,))) for ry in range(2)]
    pieces = []
    for kx in range(3):
        for ky in range(3):
            for kz in range(3):
                base = ROWS1 * (3 * kx + kz)
                at0 = base + 16 * ((ky - 1) % 5)
                at1 = base + 16 * (ky + 1)
                pieces.append(whole2[0][at0 : at0 + 16] + whole2[1][at1 : at1 + 16])
    second = jnp.concatenate(pieces + [jnp.zeros((80, 32), F32)], axis=0).T
    up1_ref[...] = dot(w2_ref[...], delta2, ((1,), (0,)))

    def folded1(x, kz, rz):
        total = None
        for kx in range(3):
            rx = x - kx
            if rx % 2 == 0 and 0 <= rx // 2 < 3:
                base = ROWS1 * (3 * kx + kz)
                lanes = slice(128 * (rx + rz), 128 * (rx + rz) + 128)
                part = up1_ref[base : base + ROWS1, lanes]
                total = part if total is None else total + part
        return total

    for x in range(7):
        for zc in range(4):
            if zc % 2 == 0:
                block = folded1(x, 1, zc // 2)
            elif zc == 1:
                block = folded1(x, 2, 0) + folded1(x, 0, 1)
            else:
                block = folded1(x, 2, 1) + down_z(folded1(x, 0, 0))
            block = jnp.concatenate([block[:48], block[48:64] + down_y(block[64:])], axis=0)
            lanes = slice(512 * x + 128 * zc, 512 * x + 128 * zc + 128)
            delta1_ref[:, lanes] = (block * slope1_ref[:, lanes]).astype(BF16)
    whole1 = dot(delta1_ref[...], cols1_ref[...], ((1,), (1,)))
    parts = []
    for _ in range(3):
        parts.append(whole1.astype(BF16))
        whole1 = whole1 - parts[-1].astype(F32)
    first = None
    copy.wait()
    for ry in range(4):
        rows = jnp.concatenate([part[16 * ry : 16 * ry + 16] for part in parts], axis=0)
        got = dot(rows, chosen_ref[ry], ((1,), (1,)))
        for at in (0, 16, 32):
            first = got[at : at + 16] if first is None else first + got[at : at + 16]

    def put(row, value):
        whole_ref[pl.ds(row, 16, stride=40), :] = value

    for x in range(4):
        for r in range(7):
            put(8 * x + r, third[16 * x : 16 * x + 16, 128 * r : 128 * r + 128])
        put(8 * x + 7, feat[16 * x : 16 * x + 16])
    for h in range(2):
        for r in range(4):
            value = second[16 * h : 16 * h + 16, 128 * r : 128 * r + 128]
            if r == 3:
                value = jnp.where(lane_iota(16) < 64, value, pltpu.roll(first, 64, 1) if h == 0 else first)
            put(32 + 4 * h + r, value)
    message_ref[...] = whole_ref[0:640, :].astype(BF16)


def passed_along(block, axis, distance):
    devices = range(lax.axis_size(axis))
    route = [(i, i + distance) for i in devices if i + distance in devices]
    return lax.ppermute(block, axis, route)


def fetch(cot_hbm, dens_hbm, out_ref, dens_ref, cot_ref, sems):
    copies = [pltpu.make_async_copy(cot_hbm, cot_ref, sems.at[0]), pltpu.make_async_copy(dens_hbm, dens_ref, sems.at[1])]
    for copy in copies:
        copy.start()
    copies[0].wait()
    out_ref[:, 0, :] = cot_ref[...].astype(F32).T
    copies[1].wait()


def regroup(got_ref, message_ref, whole_ref):
    whole_ref[0:640, :] = got_ref[...].astype(F32)
    total = whole_ref[0:40, :]
    for j in range(1, 16):
        total = total + whole_ref[40 * j : 40 * j + 40, :]
    shared = total[32:40]
    for x in range(4):
        sums = jnp.concatenate([total[8 * x : 8 * x + 8], shared], axis=0).astype(BF16)
        feat = whole_ref[pl.ds(8 * x + 7, 16, stride=40), :].astype(BF16)
        for dp in range(4):
            base = 128 * dp + 32 * x
            message_ref[base : base + 16, :] = sums
            message_ref[base + 16 : base + 32, :] = feat


def total_of(got_ref):
    total = got_ref[0:16, :].astype(F32)
    for j in range(1, 16):
        total = total + got_ref[32 * j : 32 * j + 16, :].astype(F32)
    return total


def share(got_ref, message_ref):
    total = total_of(got_ref)[8:]
    for j in range(16):
        message_ref[8 * j : 8 * j + 8, :] = total


def finish(dp_ref, got_ref, shared_ref, feat_ref, first_ref, second_ref, third_ref, whole_ref):
    whole_ref[0:CELLS, :] = shared_ref[...]
    base = pl.multiple_of(128 * dp_ref[0], 128)
    feat = [got_ref[pl.ds(base + 32 * x + 16, 16), :].astype(F32) for x in range(4)]
    feat_ref[...] = jnp.concatenate(feat, axis=0).T.astype(BF16)
    total = total_of(got_ref)[:8]
    turned = [total] + [pltpu.roll(total, 128 - 32 * q, 1) for q in range(1, 4)]
    for kx in range(3):
        for kz in range(3):
            for at, ky in enumerate((1, 2, 0)):
                b = 9 * kx + 3 * kz + at
                third_ref[9 * kx + 3 * ky + kz] = turned[b % 4][b // 4 : b // 4 + 1, :32]
    halves = []
    for h in range(2):
        halves.append(jnp.concatenate([whole_ref[pl.ds(4 * h + r, 16, stride=8), :] for r in range(4)], axis=1))
    both = jnp.concatenate(halves, axis=0).T
    second_ref[...] = both[:432]
    for c in range(4):
        h, q = c // 2, c % 2
        first_ref[:, c, :] = both[448 + 32 * q : 475 + 32 * q, 16 * h : 16 * h + 16]


def vmem(*shape, dtype=F32):
    return pltpu.VMEM(shape, dtype)


def call(kernel, out_shape, scratch=(), limit=8, **options):
    return pl.pallas_call(
        kernel,
        out_shape=out_shape,
        scratch_shapes=list(scratch),
        compiler_params=pltpu.CompilerParams(vmem_limit_bytes=limit * 1024 * 1024),
        **options,
    )


IN_HBM = pl.BlockSpec(memory_space=pltpu.HBM)
IN_VMEM = pl.BlockSpec(memory_space=pltpu.VMEM)


def in_hbm(array):
    return pltpu.with_memory_space_constraint(array, pltpu.HBM)


def in_vmem(array):
    return pltpu.with_memory_space_constraint(array, pltpu.VMEM)


def fetched(cot, dens):
    return call(
        fetch,
        (jax.ShapeDtypeStruct((64, 1, CELLS), F32), vmem(*dens.shape, dtype=BF16)),
        [vmem(CELLS, 64, dtype=BF16), pltpu.SemaphoreType.DMA((2,))],
        in_specs=[IN_HBM] * 2,
        out_specs=(IN_VMEM,) * 2,
    )(in_hbm(cot), in_hbm(dens))


def local_message(halo, dens, k1, k2, k3, cot):
    chosen = jnp.asarray(first_selection(), BF16)
    k1 = jnp.transpose(k1, (2, 3, 4, 1, 0)).reshape(27, 4, 16)
    k2 = jnp.transpose(k2, (2, 3, 4, 1, 0)).reshape(27, 16, 32)
    k3 = jnp.transpose(k3, (2, 3, 4, 1, 0)).reshape(27, 32, 64)
    arguments = (halo, k1, k2, k3, chosen)
    prepared = call(
        prepare,
        (
            vmem(15, 9 * ROWS0, CELLS, dtype=BF16),
            vmem(64, 9 * ROWS0, dtype=BF16),
            vmem(9 * ROWS1, 64, dtype=BF16),
            vmem(9 * ROWS2, 64, dtype=BF16),
            vmem(64, 9 * ROWS1, dtype=BF16),
            vmem(64, 9 * ROWS2, dtype=BF16),
        ),
        [
            *(vmem(*array.shape, dtype=BF16) for array in arguments),
            pltpu.SemaphoreType.DMA((5,)),
            vmem(1024, 1152, dtype=BF16),
            vmem(ABOVE + 64, 1024),
            vmem(27, 4, 16),
        ],
        20,
        in_specs=[IN_VMEM, pl.BlockSpec(memory_space=pl.ANY)] + [IN_HBM] * 4,
        out_specs=(IN_VMEM,) * 6,
    )(in_vmem(dens), halo, *map(in_hbm, arguments[1:]))
    return call(
        layers,
        jax.ShapeDtypeStruct((640, CELLS), BF16),
        [
            vmem(*chosen.shape, dtype=BF16),
            pltpu.SemaphoreType.DMA,
            vmem(9 * ROWS0, 3584, dtype=BF16),
            vmem(64, 3584),
            vmem(7, 5 * ROWS1, CELLS, dtype=BF16),
            vmem(9 * ROWS1, 768, dtype=BF16),
            vmem(64, 768),
            vmem(3, 3 * ROWS2, CELLS, dtype=BF16),
            vmem(9 * ROWS2, CELLS),
            vmem(9 * ROWS1, 768),
            vmem(64, 3584, dtype=BF16),
            vmem(688, CELLS),
        ],
        26,
        in_specs=[IN_VMEM] * 7 + [IN_HBM],
    )(*map(in_vmem, prepared), cot, in_hbm(chosen))


def exchanged(rows, axes):
    size = lax.axis_size(axes)
    blocks = rows.reshape(size, rows.shape[0] // size, CELLS)
    return lax.all_to_all(blocks, axes, 0, 0, tiled=True).reshape(rows.shape)


def shards(density_cubes, first_kernel, second_kernel, third_kernel, cotangent):
    shape = jax.ShapeDtypeStruct
    dens = density_cubes[0]
    halo = passed_along(dens, SPACE, 1)
    cot = jnp.transpose(cotangent, (0, 1, 3, 4, 2)).reshape(CELLS, 64)
    cot, dens = fetched(cot, dens)
    cot = lax.all_to_all(cot, SPACE, 0, 0, tiled=True)
    message = local_message(halo, dens, first_kernel, second_kernel, third_kernel, cot)
    message, dp = lax.optimization_barrier((message, lax.axis_index("dp").reshape(1)))
    got = exchanged(message, NEAR)
    got = exchanged(call(regroup, shape((512, CELLS), BF16), [vmem(688, CELLS)])(got), FAR)
    both = exchanged(call(share, shape((CELLS, CELLS), F32))(got), NEAR)
    outs = (shape((CELLS, 64), BF16), shape((27, 4, 16), F32), shape((432, 32), F32), shape((27, 1, 32), F32))
    specs = [pl.BlockSpec(memory_space=pltpu.SMEM), pl.BlockSpec(), pl.BlockSpec()]
    feat, first, second, third = call(finish, outs, [vmem(136, CELLS)], in_specs=specs)(dp, got, both)
    features = jnp.transpose(feat.reshape(1, 1, 8, 16, 64), (0, 1, 4, 2, 3))
    first_grad = jnp.transpose(first.reshape(3, 3, 3, 4, 16), (4, 3, 0, 1, 2))
    second_grad = jnp.transpose(second.reshape(3, 3, 3, 16, 32), (4, 3, 0, 1, 2))
    third_grad = jnp.transpose(third.reshape(3, 3, 3, 1, 32), (3, 4, 0, 1, 2))
    return (features, first_grad, second_grad, third_grad)


def solution(mesh):
    mesh = jax.sharding.Mesh(mesh.devices.reshape(4, 4, 2, 4, 2), ("dp",) + SPACE)
    in_specs = (
        P("dp", None, SPACE, None, None),
        P(),
        P(),
        P(),
        P("dp", SPACE, None, None, None),
    )
    out_specs = (P("dp", SPACE, None, None, None), P(), P(), P(SPACE, None, None, None, None))
    return jax.shard_map(shards, mesh=mesh, in_specs=in_specs, out_specs=out_specs, check_vma=False)
```
